128 devices in a mesh: row: 16 (over z, y_hi, core), col: 8 (over y_lo, x).
Axes of the slice: x: 4, y: 4 (y_hi: 2, y_lo: 2; y = y_hi * 2 + y_lo), z: 4, core: 2. Of those that a mesh axis runs over, the one named last changes fastest.
Arguments:
- activations: bfloat16 [2048, 8192], P('col', 'row'), may hold values from -0.13183594 to 0.13183594
- out_grad: bfloat16 [2048, 28672], P('row', 'col'), may hold values from -6 to 6
- weight: bfloat16 [8192, 28672], P('row', 'col'), may hold values from -0.0625 to 0.0625
- block_mask: int32 [128, 448], P('row', 'col'), may hold values from 0 to 1, as said below
Outputs:
- weight_grad: float32 [8192, 28672], P('row', 'col')
- input_grad: bfloat16 [2048, 8192], P('col', 'row')
The draws below stay inside these ranges and needn't reach their ends.
Inputs may be any that keep to these rules, and one draw needn't show every extreme that they name: `block_mask`: taken in tiles of 8 x 56 blocks (the blocks of one device), each tile holds at most 224 nonzero entries, and some tile holds exactly 224.
All inputs are finite; a program needn't handle non-finite values.
Results may differ from the reference program's by a relative error of at most 0.017.
Values may be sent and summed in bfloat16 or wider, within the bound.
A program may use at most 128 MiB of HBM per device.

```python
import jax
import jax.numpy as jnp
from jax import lax

D = 8192
FF = 28672
BLK = 64
TOKENS = 2048
NBD = 128
NBF = 448
TILE_R = 8
TILE_C = 56
CAP = 224
N_ROW = 16
N_COL = 8


def draw_block_mask(key, part):
    key = jax.random.fold_in(key, 7)
    key_count, key_pos, key_perm = jax.random.split(key, 3)
    tiles = N_ROW * N_COL
    per_tile = TILE_R * TILE_C
    counts = jax.random.randint(key_count, (tiles,), per_tile // 8, CAP + 1)
    fullest = jax.random.randint(key_pos, (), 0, tiles)
    counts = jnp.where(jnp.arange(tiles) == fullest, CAP, counts)
    keys = jax.random.split(key_perm, tiles)

    def one_tile(tile_key, count):
        ones = (jnp.arange(per_tile) < count).astype(jnp.int32)
        return jax.random.permutation(tile_key, ones)
    flat = jax.vmap(one_tile)(keys, counts)
    grid = flat.reshape(N_ROW, N_COL, TILE_R, TILE_C).transpose(0, 2, 1, 3)
    return grid.reshape(NBD, NBF).astype(jnp.int32)


def level_of(own_key, shape, cuts, least, top_value):
    def one(dim, blocks):
        steps = jax.random.uniform(jax.random.fold_in(jax.random.fold_in(own_key, 6), dim), (blocks,), jnp.float32, least / len(cuts), top_value / len(cuts))
        return jnp.repeat(jnp.exp(steps), shape[dim] // blocks).reshape((-1,) + (1,) * (len(shape) - dim - 1))

    level = one(*cuts[0])
    for cut in cuts[1:]:
        level = level * one(*cut)
    return level


def gaussian(stream_key, dims, deviation, bound, cuts=(), kind=jnp.bfloat16):
    factor_of = level_of(stream_key, dims, cuts, -0.22, 0.18) if cuts else 1.0
    array = jax.random.normal(stream_key, dims, jnp.float32) * deviation * factor_of
    return jnp.minimum(jnp.maximum(array, -bound), bound).astype(kind)


def setup_inputs(seed: int = 0) -> dict:
    seeds = jax.random.split(jax.random.key(seed), 5)
    return {
        "activations": gaussian(seeds[0], (TOKENS, D), (TOKENS ** -0.5), 0.13183594, ((0, 8), (1, 16))),
        "out_grad": gaussian(seeds[1], (TOKENS, FF), 1.0, 6.0, ((0, 16), (1, 8))),
        "weight": gaussian(seeds[2], (D, FF), (FF // 4) ** -0.5, 0.0625, ((0, 16), (1, 8))),
        "block_mask": draw_block_mask(jax.random.fold_in(seeds[4], 71), 0),
    }


def reference(activations, out_grad, weight, block_mask):
    mask_f = block_mask.astype(jnp.float32)[:, None, :, None]
    x_f = activations.astype(jnp.float32)
    dy_f = out_grad.astype(jnp.float32)
    grad = jnp.dot(x_f.T, dy_f, precision=lax.Precision.HIGHEST, preferred_element_type=jnp.float32)
    grad = (grad.reshape(NBD, BLK, NBF, BLK) * mask_f).reshape(D, FF)
    masked = (weight.astype(jnp.float32).reshape(NBD, BLK, NBF, BLK) * mask_f).reshape(D, FF)
    width_group = FF // N_COL
    total = jnp.zeros((TOKENS, D), jnp.float32)
    for group_index in range(N_COL):
        first = group_index * width_group
        partial_sum = jnp.dot(dy_f[:, first:first + width_group], masked[:, first:first + width_group].T, precision=lax.Precision.HIGHEST, preferred_element_type=jnp.float32)
        rounded = lax.optimization_barrier(partial_sum.astype(jnp.bfloat16))
        total = total + rounded.astype(jnp.float32)
    return grad, total.astype(jnp.bfloat16)
```

```python
import functools

import jax
import jax.numpy as jnp
from jax import lax
from jax.experimental import pallas as pl
from jax.experimental.pallas import tpu as pltpu
from jax.sharding import PartitionSpec as P

BLK = 64
STEPS = 8
ROWS = 16
AHEAD = 3
MESH = pl.DeviceIdType.MESH

M1, OWN, P1, Z2, Y, YP1, YZ2, YM1 = range(8)
S_ZP, S_ZM, S_Y, S_FWD, S_YZP, S_YZM, S_Y2 = range(7)


def slot_of(dz, dh):
    return 4 * dh + (dz + 1 - dh) % 4


def comm_kernel(
    x_ref, dy_ref, w_ref, mask_ref,
    acc_ref, ig_ref,
    dyf, xp, xt, wv, wmt, mcols, dxb, rsb, ysend, yland,
    s_piece, r_piece, s_core, r_core, s_x, r_x, s_rs, r_rs, s_y, r_y, loc,
):
    row, col = lax.axis_index("row"), lax.axis_index("col")
    core = lax.rem(row, 2)
    h = lax.rem(lax.div(row, 2), 2)
    z = lax.div(row, 4)
    x = lax.rem(col, 4)
    yl = lax.div(col, 4)

    def row_id(z_, h_, c_):
        return (z_ * 2 + h_) * 2 + c_

    zp = (row_id(lax.rem(z + 1, 4), h, core), col)
    zm = (row_id(lax.rem(z + 3, 4), h, core), col)
    yp = (row_id(z, 1 - h, core), col)
    other_core = (row_id(z, h, 1 - core), col)
    yn = (row, (1 - yl) * 4 + x)

    def xpeer(o):
        return (row, yl * 4 + lax.rem(x + o, 4))

    barrier = pltpu.get_barrier_semaphore()
    partners = [zp, zm, yp, other_core, yn, xpeer(1), xpeer(2), xpeer(3)]
    for dev in partners:
        pl.semaphore_signal(barrier, inc=1, device_id=dev, device_id_type=MESH)

    own_dy = pltpu.make_async_copy(dy_ref, dyf.at[:, core, OWN], loc.at[0])
    own_dy.start()
    w_copy = pltpu.make_async_copy(w_ref, wv, loc.at[1])
    w_copy.start()

    def x_slot(yl_):
        j = yl_ * 4 + x
        dz = lax.rem(lax.div(j, 2) + 4 - z, 4)
        dh = lax.rem(lax.rem(j, 2) + 2 - h, 2)
        return 4 * dh + lax.rem(dz + 5 - dh, 4)

    own_x = [pltpu.make_async_copy(x_ref.at[c], xp.at[:, c, x_slot(yl)], loc.at[2 + c]) for c in range(2)]
    for cp in own_x:
        cp.start()

    pl.semaphore_wait(barrier, len(partners))

    def remote(src, dst, ss, rs, dev):
        return pltpu.make_async_remote_copy(
            src_ref=src, dst_ref=dst, send_sem=ss, recv_sem=rs, device_id=dev, device_id_type=MESH
        )

    def piece(kind, p):
        src_slot, dst_slot, dev = {
            S_ZP: (None, M1, zp),
            S_ZM: (None, P1, zm),
            S_Y: (None, Y, yp),
            S_YZP: (Y, YM1, zp),
            S_YZM: (Y, YP1, zm),
            S_Y2: (Z2, YZ2, yp),
        }[kind]
        src = dy_ref.at[p] if src_slot is None else dyf.at[p, core, src_slot]
        return remote(src, dyf.at[p, core, dst_slot], s_piece.at[kind, p], r_piece.at[dst_slot, p], dev)

    def fwd(p, up):
        src = dyf.at[p, core, M1 if up else P1]
        return remote(src, dyf.at[p, core, Z2], s_piece.at[S_FWD, p], r_piece.at[Z2, p], zp if up else zm)

    def to_core(g, p):
        lo, n = ((0, 3), (3, 5))[g]
        there = dyf.at[p, core, pl.ds(lo, n)]
        return remote(there, there, s_core.at[g, p], r_core.at[g, p], other_core)

    def from_core(g, p):
        lo, n = ((0, 3), (3, 5))[g]
        here = dyf.at[p, 1 - core, pl.ds(lo, n)]
        return remote(here, here, s_core.at[g, p], r_core.at[g, p], other_core)

    def own_sends(p):
        for kind in (S_ZP, S_ZM, S_Y):
            piece(kind, p).start()

    def x_send(o, c):
        there = xp.at[:, c, x_slot(yl)]
        return remote(x_ref.at[c], there, s_x.at[0, o, c], r_x.at[0, o, c], xpeer(o) if o else yn)

    def x_hand(o, c):
        there = xp.at[:, c, x_slot(1 - yl)]
        return remote(there, there, s_x.at[1, o, c], r_x.at[1, o, c], xpeer(o))

    dzp_own = lax.rem(lax.div(x, 2) + 4 - z, 2)
    dh_own = lax.rem(lax.rem(x, 2) + 2 - h, 2)
    cls_own = dh_own * 2 + dzp_own
    keep = lax.rem(yl + lax.div(lax.rem(z + dzp_own, 4), 2), 2)

    def cls_dest(cls):
        dh, dzp = cls // 2, cls % 2
        return 2 * lax.rem(z + dzp, 2) + lax.rem(h + dh, 2)

    def rs_send(cls, p):
        xs = cls_dest(cls)
        o = lax.rem(x + 4 - xs + 3, 4)
        return remote(dxb.at[p, cls], rsb.at[o, p], s_rs.at[cls, p], r_rs.at[o, p], (row, yl * 4 + xs))

    def rs_recv(o, p):
        return remote(rsb.at[o, p], rsb.at[o, p], s_rs.at[0, p], r_rs.at[o, p], xpeer(1))

    def y_send(p):
        return remote(ysend.at[p], yland.at[p], s_y.at[p], r_y.at[p], yn)

    for p in range(AHEAD):
        own_sends(p)
    for c in range(2):
        for o in range(4):
            x_send(o, c).start()

    d_loc, f_loc = wv.shape
    nbr, nbc = mask_ref.shape
    tile = 512
    n_tiles = f_loc // tile
    mask_bf = mask_ref[...].astype(jnp.bfloat16)

    def spread(i, _):
        cols = pl.ds(pl.multiple_of(i * tile, tile), tile)
        block = lax.broadcasted_iota(jnp.int32, (nbc, tile), 0)
        first = block * BLK - i * tile
        lane = lax.broadcasted_iota(jnp.int32, (nbc, tile), 1)
        hit = jnp.logical_and(lane >= first, lane < first + BLK)
        pick = jnp.where(hit, 1.0, 0.0).astype(jnp.bfloat16)
        mcols[:, cols] = jnp.dot(mask_bf, pick, preferred_element_type=jnp.float32)
        return 0

    lax.fori_loop(0, n_tiles, spread, 0)
    w_copy.wait()

    def mask_w(i, _):
        cols = pl.ds(pl.multiple_of(i * tile, tile), tile)
        upper = lax.broadcasted_iota(jnp.int32, (2 * BLK, tile), 0) < BLK
        for b in range(d_loc // (2 * BLK)):
            m = jnp.where(upper, mcols[2 * b : 2 * b + 1, cols], mcols[2 * b + 1 : 2 * b + 2, cols])
            wm = wv[b * 2 * BLK : (b + 1) * 2 * BLK, cols] * m.astype(jnp.bfloat16)
            wmt[cols, b * 2 * BLK : (b + 1) * 2 * BLK] = wm.T
        return 0

    lax.fori_loop(0, n_tiles, mask_w, 0)
    own_dy.wait()

    def wgrad(b, first, last):
        span = xt.shape[1]
        xt[...] = xp[pl.ds(2 * b, 2)].reshape(span, d_loc).T

        def one(i, _):
            cols = pl.ds(pl.multiple_of(i * tile, tile), tile)
            dy2 = dyf[pl.ds(2 * b, 2), :, :, :, cols].reshape(span, tile)
            part = jnp.dot(xt[...], dy2, preferred_element_type=jnp.float32)
            if not first:
                part = part + acc_ref[:, cols]
            if last:
                for i_b in range(nbr):
                    rows = slice(i_b * BLK, (i_b + 1) * BLK)
                    acc_ref[rows, cols] = part[rows] * mcols[i_b : i_b + 1, cols]
            else:
                acc_ref[:, cols] = part
            return 0

        lax.fori_loop(0, n_tiles, one, 0)

    def in_range(s, lag):
        return jnp.logical_and(s >= lag, s < STEPS + lag)

    def step(s, _):
        @pl.when(s < STEPS)
        def _():
            piece(S_ZP, s).wait_recv()
            piece(S_ZM, s).wait_recv()

            @pl.when(s < STEPS - AHEAD)
            def _():
                own_sends(s + AHEAD)

            @pl.when(lax.rem(s, 2) == 0)
            def _():
                fwd(s, True).start()

            @pl.when(lax.rem(s, 2) == 1)
            def _():
                fwd(s, False).start()

            to_core(0, s).start()
            piece(S_Y, s).wait_recv()
            piece(S_YZP, s).start()
            piece(S_YZM, s).start()

        @pl.when(s == 0)
        def _():
            for c in range(2):
                x_send(0, c).wait_recv()
                for o in range(1, 4):
                    x_hand(o, c).start()

        @pl.when(in_range(s, 1))
        def _():
            q = s - 1
            fwd(q, True).wait_recv()
            piece(S_Y2, q).start()
            piece(S_YZP, q).wait_recv()
            piece(S_YZM, q).wait_recv()

        @pl.when(in_range(s, 2))
        def _():
            q = s - 2
            piece(S_Y2, q).wait_recv()
            to_core(1, q).start()

        @pl.when(in_range(s, 3))
        def _():
            q = s - 3
            from_core(0, q).wait_recv()
            from_core(1, q).wait_recv()
            part = jnp.dot(
                dyf[q].reshape(16 * ROWS, f_loc), wmt[...], preferred_element_type=jnp.float32
            ).astype(jnp.bfloat16)
            for cls in range(4):
                dh, dzp = cls // 2, cls % 2
                for m in range(2):
                    slot = slot_of(dzp + 2 * m, dh)
                    for c in range(2):
                        at = (c * 8 + slot) * ROWS
                        dxb[q, cls, m, c] = part[at : at + ROWS]
            for cls in range(4):

                @pl.when(cls_dest(cls) != x)
                def _():
                    rs_send(cls, q).start()

            @pl.when(q == 1)
            def _():
                for c in range(2):
                    own_x[c].wait()
                    for o in range(1, 4):
                        x_send(o, c).wait_recv()
                        x_hand(o, c).wait_recv()
                wgrad(0, True, False)

            @pl.when(jnp.logical_and(lax.rem(q, 2) == 1, jnp.logical_and(q > 1, q < STEPS - 1)))
            def _():
                wgrad(lax.div(q, 2), False, False)

            @pl.when(q == STEPS - 1)
            def _():
                wgrad(STEPS // 2 - 1, False, True)

        @pl.when(in_range(s, 4))
        def _():
            q = s - 4
            for o in range(3):
                rs_recv(o, q).wait_recv()

            def total(m):
                t = dxb[q, cls_own, m].astype(jnp.float32)
                for o in range(3):
                    t = t + rsb[o, q, m].astype(jnp.float32)
                return t

            ysend[q] = total(1 - keep).astype(jnp.bfloat16)
            y_send(q).start()

        @pl.when(in_range(s, 5))
        def _():
            q = s - 5
            t = dxb[q, cls_own, keep].astype(jnp.float32)
            for o in range(3):
                t = t + rsb[o, q, keep].astype(jnp.float32)
            y_send(q).wait_recv()
            t = (t + yland[q].astype(jnp.float32)).astype(jnp.bfloat16)
            for c in range(2):
                ig_ref[c, q] = t[c]

        return 0

    lax.fori_loop(0, STEPS + 5, step, 0)

    def drain(p, _):
        for kind in (S_ZP, S_ZM, S_Y, S_YZP, S_YZM, S_Y2):
            piece(kind, p).wait_send()
        fwd(p, True).wait_send()
        for g in range(2):
            to_core(g, p).wait_send()
        for cls in range(4):

            @pl.when(cls_dest(cls) != x)
            def _():
                rs_send(cls, p).wait_send()

        y_send(p).wait_send()
        return 0

    lax.fori_loop(0, STEPS, drain, 0)
    for c in range(2):
        for o in range(4):
            x_send(o, c).wait_send()
            if o:
                x_hand(o, c).wait_send()


def write_kernel(acc_ref, ig_ref, wg_ref, ig_out, sems):
    a = pltpu.make_async_copy(acc_ref, wg_ref, sems.at[0])
    b = pltpu.make_async_copy(ig_ref, ig_out, sems.at[1])
    a.start()
    b.start()
    a.wait()
    b.wait()


def local(activations, out_grad, weight, block_mask):
    t_loc, d_loc = activations.shape
    s_loc, f_loc = out_grad.shape
    bf, f32 = jnp.bfloat16, jnp.float32
    dma = pltpu.SemaphoreType.DMA
    hbm = pl.BlockSpec(memory_space=pltpu.HBM)
    vmem = pl.BlockSpec(memory_space=pltpu.VMEM)
    acc, ig = pl.pallas_call(
        comm_kernel,
        out_shape=(
            pltpu.VMEM((d_loc, f_loc), f32),
            pltpu.VMEM((2, STEPS, ROWS, d_loc), bf),
        ),
        in_specs=[hbm, hbm, hbm, vmem],
        out_specs=(vmem, vmem),
        scratch_shapes=[
            pltpu.VMEM((STEPS, 2, 8, ROWS, f_loc), bf),
            pltpu.VMEM((STEPS, 2, 8, ROWS, d_loc), bf),
            pltpu.VMEM((d_loc, 32 * ROWS), bf),
            pltpu.VMEM((d_loc, f_loc), bf),
            pltpu.VMEM((f_loc, d_loc), bf),
            pltpu.VMEM((block_mask.shape[0], f_loc), f32),
            pltpu.VMEM((STEPS, 4, 2, 2, ROWS, d_loc), bf),
            pltpu.VMEM((3, STEPS, 2, 2, ROWS, d_loc), bf),
            pltpu.VMEM((STEPS, 2, ROWS, d_loc), bf),
            pltpu.VMEM((STEPS, 2, ROWS, d_loc), bf),
            dma((7, STEPS)),
            dma((8, STEPS)),
            dma((2, STEPS)),
            dma((2, STEPS)),
            dma((2, 4, 2)),
            dma((2, 4, 2)),
            dma((4, STEPS)),
            dma((3, STEPS)),
            dma((STEPS,)),
            dma((STEPS,)),
            dma((4,)),
        ],
        compiler_params=pltpu.CompilerParams(
            collective_id=0, has_side_effects=True, vmem_limit_bytes=46 * 2**20
        ),
        name="gather_multiply_reduce",
    )(
        activations.reshape(2, STEPS, ROWS, d_loc),
        out_grad.reshape(STEPS, ROWS, f_loc),
        weight,
        block_mask,
    )
    wg, igo = pl.pallas_call(
        write_kernel,
        out_shape=(
            jax.ShapeDtypeStruct((d_loc, f_loc), f32),
            jax.ShapeDtypeStruct((2, STEPS, ROWS, d_loc), bf),
        ),
        in_specs=[vmem, vmem],
        out_specs=(pl.BlockSpec(memory_space=pl.ANY), pl.BlockSpec(memory_space=pl.ANY)),
        scratch_shapes=[dma((2,))],
        compiler_params=pltpu.CompilerParams(vmem_limit_bytes=1 * 2**20),
        name="write_out",
    )(acc, ig)
    return wg, igo.reshape(t_loc, d_loc)


def solution(mesh):
    in_specs = (P("col", "row"), P("row", "col"), P("row", "col"), P("row", "col"))
    out_specs = (P("row", "col"), P("col", "row"))
    return jax.shard_map(local, mesh=mesh, in_specs=in_specs, out_specs=out_specs, check_vma=False)
```

```python
import functools

import jax
import jax.numpy as jnp
from jax import lax
from jax.experimental import pallas as pl
from jax.experimental.pallas import tpu as pltpu
from jax.sharding import PartitionSpec as P

BLK = 64
STEPS = 8
ROWS = 16
AHEAD = 2
LAG_YZ2, LAG_DX = 2, 2
MESH = pl.DeviceIdType.MESH

M1, OWN, P1, Y, Z2, YP1, YZ2, YM1 = range(8)
CORE_GROUPS = ((0, 4), (4, 2), (6, 2))
S_ZP, S_ZM, S_Y, S_FWD, S_YZP, S_YZM, S_Y2 = range(7)


def slot_of(dz, dh):
    return ((OWN, P1, Z2, M1), (Y, YP1, YZ2, YM1))[dh][dz]


def comm_kernel(
    x_ref, dy_ref, w_ref, mask_hbm,
    acc_ref, ig_ref,
    mask_ref, dyf, xp, xt, wv, wmt, mcols, dxb, rsb, ysend, yland,
    s_piece, r_piece, s_core, r_core, s_x, r_x, s_rs, r_rs, s_half, r_half, s_y, r_y, loc,
):
    row, col = lax.axis_index("row"), lax.axis_index("col")
    core = lax.rem(row, 2)
    h = lax.rem(lax.div(row, 2), 2)
    z = lax.div(row, 4)
    x = lax.rem(col, 4)
    yl = lax.div(col, 4)

    def row_id(z_, h_, c_):
        return (z_ * 2 + h_) * 2 + c_

    zp = (row_id(lax.rem(z + 1, 4), h, core), col)
    zm = (row_id(lax.rem(z + 3, 4), h, core), col)
    yp = (row_id(z, 1 - h, core), col)
    other_core = (row_id(z, h, 1 - core), col)
    yn = (row, (1 - yl) * 4 + x)

    def xpeer(o):
        return (row, yl * 4 + lax.rem(x + o, 4))

    barrier = pltpu.get_barrier_semaphore()
    partners = [zp, zm, yp, other_core, yn, xpeer(1), xpeer(2), xpeer(3)]
    for dev in partners:
        pl.semaphore_signal(barrier, inc=1, device_id=dev, device_id_type=MESH)

    own_dy = pltpu.make_async_copy(dy_ref, dyf.at[:, core, OWN], loc.at[0])
    own_dy.start()
    w_copy = pltpu.make_async_copy(w_ref, wv, loc.at[1])
    w_copy.start()
    mask_copy = pltpu.make_async_copy(mask_hbm, mask_ref, loc.at[4])
    mask_copy.start()

    def x_slot(yl_):
        j = yl_ * 4 + x
        dz = lax.rem(lax.div(j, 2) + 4 - z, 4)
        dh = lax.rem(lax.rem(j, 2) + 2 - h, 2)
        near = lax.rem(dz + 1, 4) + lax.div(dz * (dz - 1) * (3 - dz), 2)
        far = 3 + dz + lax.div(dz + 2, 3)
        return near + dh * (far - near)

    own_x = [pltpu.make_async_copy(x_ref.at[c], xp.at[:, c, x_slot(yl)], loc.at[2 + c]) for c in range(2)]
    for cp in own_x:
        cp.start()

    pl.semaphore_wait(barrier, len(partners))

    def remote(src, dst, ss, rs, dev):
        return pltpu.make_async_remote_copy(
            src_ref=src, dst_ref=dst, send_sem=ss, recv_sem=rs, device_id=dev, device_id_type=MESH
        )

    def piece(kind, p):
        src_slot, dst_slot, dev = {
            S_ZP: (None, M1, zp),
            S_ZM: (None, P1, zm),
            S_Y: (None, Y, yp),
            S_YZP: (Y, YM1, zp),
            S_YZM: (Y, YP1, zm),
            S_Y2: (Z2, YZ2, yp),
        }[kind]
        src = dy_ref.at[p] if src_slot is None else dyf.at[p, core, src_slot]
        return remote(src, dyf.at[p, core, dst_slot], s_piece.at[kind, p], r_piece.at[dst_slot, p], dev)

    def fwd(p, up):
        src = dyf.at[p, core, M1 if up else P1]
        return remote(src, dyf.at[p, core, Z2], s_piece.at[S_FWD, p], r_piece.at[Z2, p], zp if up else zm)

    def to_core(g, p):
        lo, n = CORE_GROUPS[g]
        there = dyf.at[p, core, pl.ds(lo, n)]
        return remote(there, there, s_core.at[g, p], r_core.at[g, p], other_core)

    def from_core(g, p):
        lo, n = CORE_GROUPS[g]
        here = dyf.at[p, 1 - core, pl.ds(lo, n)]
        return remote(here, here, s_core.at[g, p], r_core.at[g, p], other_core)

    def own_sends(p):
        for kind in (S_ZP, S_ZM, S_Y):
            piece(kind, p).start()

    def x_send(o, c):
        there = xp.at[:, c, x_slot(yl)]
        return remote(x_ref.at[c], there, s_x.at[0, o, c], r_x.at[0, o, c], xpeer(o) if o else yn)

    def x_hand(o, c):
        there = xp.at[:, c, x_slot(1 - yl)]
        return remote(there, there, s_x.at[1, o, c], r_x.at[1, o, c], xpeer(o))

    dzp_own = lax.rem(lax.div(x, 2) + 4 - z, 2)
    dh_own = lax.rem(lax.rem(x, 2) + 2 - h, 2)
    cls_own = dh_own * 2 + dzp_own
    keep = lax.rem(yl + lax.div(lax.rem(z + dzp_own, 4), 2), 2)

    def cls_dest(cls):
        dh, dzp = cls // 2, cls % 2
        return 2 * lax.rem(z + dzp, 2) + lax.rem(h + dh, 2)

    def rs_send(cls, p):
        xs = cls_dest(cls)
        o = lax.rem(x + 4 - xs + 3, 4)
        return remote(dxb.at[p, cls], rsb.at[o, p], s_rs.at[cls, p], r_rs.at[o, p], (row, yl * 4 + xs))

    def rs_recv(o, p):
        return remote(rsb.at[o, p], rsb.at[o, p], s_rs.at[0, p], r_rs.at[o, p], xpeer(1))

    def rs_send_half(cls, m, p):
        xs = cls_dest(cls)
        o = lax.rem(x + 4 - xs + 3, 4)
        return remote(
            dxb.at[p, cls, m], rsb.at[o, p, m], s_half.at[cls, m], r_half.at[o, m], (row, yl * 4 + xs)
        )

    def rs_recv_half(o, m, p):
        return remote(rsb.at[o, p, m], rsb.at[o, p, m], s_half.at[0, 0], r_half.at[o, m], xpeer(1))

    def y_send(p):
        return remote(ysend.at[p], yland.at[p], s_y.at[p], r_y.at[p], yn)

    for p in range(AHEAD):
        own_sends(p)
    for c in range(2):
        for o in range(4):
            x_send(o, c).start()

    d_loc, f_loc = wv.shape
    nbr, nbc = mask_ref.shape
    tile = 512
    n_tiles = f_loc // tile
    mask_copy.wait()
    mask_bf = mask_ref[...].astype(jnp.bfloat16)

    def spread(i, _):
        cols = pl.ds(pl.multiple_of(i * tile, tile), tile)
        block = lax.broadcasted_iota(jnp.int32, (nbc, tile), 0)
        first = block * BLK - i * tile
        lane = lax.broadcasted_iota(jnp.int32, (nbc, tile), 1)
        hit = jnp.logical_and(lane >= first, lane < first + BLK)
        pick = jnp.where(hit, 1.0, 0.0).astype(jnp.bfloat16)
        mcols[:, cols] = jnp.dot(mask_bf, pick, preferred_element_type=jnp.float32)
        return 0

    lax.fori_loop(0, n_tiles, spread, 0)
    w_copy.wait()

    def mask_w(i, _):
        cols = pl.ds(pl.multiple_of(i * tile, tile), tile)
        upper = lax.broadcasted_iota(jnp.int32, (2 * BLK, tile), 0) < BLK
        for b in range(d_loc // (2 * BLK)):
            m = jnp.where(upper, mcols[2 * b : 2 * b + 1, cols], mcols[2 * b + 1 : 2 * b + 2, cols])
            wm = wv[b * 2 * BLK : (b + 1) * 2 * BLK, cols] * m.astype(jnp.bfloat16)
            wmt[cols, b * 2 * BLK : (b + 1) * 2 * BLK] = wm.T
        return 0

    lax.fori_loop(0, n_tiles, mask_w, 0)
    own_dy.wait()

    def wgrad(b, first, last, lo=0, hi=n_tiles):
        span = xt.shape[1]
        if lo == 0:
            xt[...] = xp[pl.ds(2 * b, 2)].reshape(span, d_loc).T

        def one(i, _):
            cols = pl.ds(pl.multiple_of(i * tile, tile), tile)
            dy2 = dyf[pl.ds(2 * b, 2), :, :, :, cols].reshape(span, tile)
            part = jnp.dot(xt[...], dy2, preferred_element_type=jnp.float32)
            if not first:
                part = part + acc_ref[:, cols]
            if last:
                for i_b in range(nbr):
                    rows = slice(i_b * BLK, (i_b + 1) * BLK)
                    acc_ref[rows, cols] = part[rows] * mcols[i_b : i_b + 1, cols]
            else:
                acc_ref[:, cols] = part
            return 0

        lax.fori_loop(lo, hi, one, 0)

    def dx_rows(q, lo, n):
        part = jnp.dot(
            dyf[q, :, lo : lo + n].reshape(2 * n * ROWS, f_loc), wmt[...], preferred_element_type=jnp.float32
        ).astype(jnp.bfloat16)
        for cls in range(4):
            dh, dzp = cls // 2, cls % 2
            for m in range(2):
                slot = slot_of(dzp + 2 * m, dh)
                if not lo <= slot < lo + n:
                    continue
                for c in range(2):
                    at = (c * n + slot - lo) * ROWS
                    dxb[q, cls, m, c] = part[at : at + ROWS]
                if n < 8:

                    @pl.when(cls_dest(cls) != x)
                    def _():
                        rs_send_half(cls, m, q).start()

    def dx_step(q):
        for g in range(3):
            from_core(g, q).wait_recv()
        dx_rows(q, 0, 8)
        for cls in range(4):

            @pl.when(cls_dest(cls) != x)
            def _():
                rs_send(cls, q).start()

    def rs_total(q, m):
        t = dxb[q, cls_own, m].astype(jnp.float32)
        for o in range(3):
            t = t + rsb[o, q, m].astype(jnp.float32)
        return t

    def rs_wait(q, m):
        for o in range(3):
            if isinstance(q, int) and q == STEPS - 1:
                rs_recv_half(o, m, q).wait_recv()
            else:
                rs_recv(o, q).wait_recv()

    def rs_along_y(q):
        rs_wait(q, 1 - keep)
        ysend[q] = rs_total(q, 1 - keep).astype(jnp.bfloat16)
        y_send(q).start()

    def rs_finish(q):
        if isinstance(q, int) and q == STEPS - 1:
            rs_wait(q, keep)
        t = rs_total(q, keep)
        y_send(q).wait_recv()
        t = (t + yland[q].astype(jnp.float32)).astype(jnp.bfloat16)
        for c in range(2):
            ig_ref[c, q] = t[c]

    def neighbours(p, more):
        piece(S_ZP, p).wait_recv()
        piece(S_ZM, p).wait_recv()

        @pl.when(lax.rem(p, 2) == 0)
        def _():
            fwd(p, True).start()

        @pl.when(lax.rem(p, 2) == 1)
        def _():
            fwd(p, False).start()

        piece(S_Y, p).wait_recv()
        piece(S_YZP, p).start()
        piece(S_YZM, p).start()
        to_core(0, p).start()

        @pl.when(more)
        def _():
            own_sends(p + AHEAD)

    def second(p):
        fwd(p, True).wait_recv()
        piece(S_Y2, p).start()

    def second_core(p):
        piece(S_YZM, p).wait_recv()
        to_core(1, p).start()

    def third(p):
        piece(S_YZP, p).wait_recv()
        piece(S_Y2, p).wait_recv()
        to_core(2, p).start()

    def step(s, _):
        neighbours(s, s < STEPS - AHEAD)

        @pl.when(s == 0)
        def _():
            for c in range(2):
                x_send(0, c).wait_recv()
                for o in range(1, 4):
                    x_hand(o, c).start()

        @pl.when(s >= LAG_YZ2)
        def _():
            third(s - LAG_YZ2)

        @pl.when(s >= 1)
        def _():
            second(s - 1)
            second_core(s - 1)

        @pl.when(s >= LAG_DX)
        def _():
            q = s - LAG_DX
            dx_step(q)

            @pl.when(q == 2)
            def _():
                for c in range(2):
                    own_x[c].wait()
                    for o in range(1, 4):
                        x_send(o, c).wait_recv()
                        x_hand(o, c).wait_recv()
                wgrad(0, True, False, 0, 4)

            @pl.when(q == 3)
            def _():
                wgrad(0, True, False, 4, n_tiles)

            @pl.when(q == 4)
            def _():
                wgrad(1, False, False, 0, 4)

            @pl.when(q == 5)
            def _():
                wgrad(1, False, False, 4, n_tiles)

        @pl.when(s >= LAG_DX + 1)
        def _():
            rs_along_y(s - LAG_DX - 1)

        @pl.when(s >= LAG_DX + 2)
        def _():
            rs_finish(s - LAG_DX - 2)

        return 0

    lax.fori_loop(0, STEPS, step, 0)
    last = STEPS - 1
    third(last - 1)
    second(last)
    second_core(last)
    from_core(0, last).wait_recv()
    dx_rows(last, 0, 4)
    dx_step(last - 1)
    rs_along_y(last - 2)
    rs_finish(last - 3)
    third(last)
    wgrad(2, False, False, 0, 3)
    from_core(1, last).wait_recv()
    from_core(2, last).wait_recv()
    dx_rows(last, 4, 4)
    rs_along_y(last - 1)
    rs_finish(last - 2)
    wgrad(2, False, False, 3, n_tiles)
    rs_along_y(last)
    rs_finish(last - 1)
    wgrad(3, False, True)
    rs_finish(last)

    def drain(p, _):
        for kind in (S_ZP, S_ZM, S_Y, S_YZP, S_YZM, S_Y2):
            piece(kind, p).wait_send()
        fwd(p, True).wait_send()
        for g in range(3):
            to_core(g, p).wait_send()
        y_send(p).wait_send()
        return 0

    def drain_rs(p, _):
        for cls in range(4):

            @pl.when(cls_dest(cls) != x)
            def _():
                rs_send(cls, p).wait_send()

        return 0

    lax.fori_loop(0, STEPS, drain, 0)
    lax.fori_loop(0, STEPS - 1, drain_rs, 0)
    for cls in range(4):

        @pl.when(cls_dest(cls) != x)
        def _():
            for m in range(2):
                rs_send_half(cls, m, STEPS - 1).wait_send()

    for c in range(2):
        for o in range(4):
            x_send(o, c).wait_send()
            if o:
                x_hand(o, c).wait_send()


def write_kernel(acc_ref, ig_ref, wg_ref, ig_out, sems):
    parts = 8
    rows = acc_ref.shape[0] // parts
    copies = [pltpu.make_async_copy(ig_ref, ig_out, sems.at[parts])]
    for i in range(parts):
        part = pl.ds(i * rows, rows)
        copies.append(pltpu.make_async_copy(acc_ref.at[part], wg_ref.at[part], sems.at[i]))
    for cp in copies:
        cp.start()
    for cp in copies:
        cp.wait()


def local(activations, out_grad, weight, block_mask):
    t_loc, d_loc = activations.shape
    s_loc, f_loc = out_grad.shape
    bf, f32 = jnp.bfloat16, jnp.float32
    dma = pltpu.SemaphoreType.DMA
    hbm = pl.BlockSpec(memory_space=pltpu.HBM)
    vmem = pl.BlockSpec(memory_space=pltpu.VMEM)
    acc, ig = pl.pallas_call(
        comm_kernel,
        out_shape=(
            pltpu.VMEM((d_loc, f_loc), f32),
            pltpu.VMEM((2, STEPS, ROWS, d_loc), bf),
        ),
        in_specs=[hbm] * 4,
        out_specs=(vmem, vmem),
        scratch_shapes=[
            pltpu.VMEM(block_mask.shape, jnp.int32),
            pltpu.VMEM((STEPS, 2, 8, ROWS, f_loc), bf),
            pltpu.VMEM((STEPS, 2, 8, ROWS, d_loc), bf),
            pltpu.VMEM((d_loc, 32 * ROWS), bf),
            pltpu.VMEM((d_loc, f_loc), bf),
            pltpu.VMEM((f_loc, d_loc), bf),
            pltpu.VMEM((block_mask.shape[0], f_loc), f32),
            pltpu.VMEM((STEPS, 4, 2, 2, ROWS, d_loc), bf),
            pltpu.VMEM((3, STEPS, 2, 2, ROWS, d_loc), bf),
            pltpu.VMEM((STEPS, 2, ROWS, d_loc), bf),
            pltpu.VMEM((STEPS, 2, ROWS, d_loc), bf),
            dma((7, STEPS)),
            dma((8, STEPS)),
            dma((3, STEPS)),
            dma((3, STEPS)),
            dma((2, 4, 2)),
            dma((2, 4, 2)),
            dma((4, STEPS)),
            dma((3, STEPS)),
            dma((4, 2)),
            dma((3, 2)),
            dma((STEPS,)),
            dma((STEPS,)),
            dma((5,)),
        ],
        compiler_params=pltpu.CompilerParams(
            collective_id=0, has_side_effects=True, vmem_limit_bytes=46 * 2**20
        ),
        name="gather_multiply_reduce",
    )(
        *(
            pltpu.with_memory_space_constraint(a, pltpu.HBM)
            for a in (
                activations.reshape(2, STEPS, ROWS, d_loc),
                out_grad.reshape(STEPS, ROWS, f_loc),
                weight,
                block_mask,
            )
        )
    )
    wg, igo = pl.pallas_call(
        write_kernel,
        out_shape=(
            jax.ShapeDtypeStruct((d_loc, f_loc), f32),
            jax.ShapeDtypeStruct((2, STEPS, ROWS, d_loc), bf),
        ),
        in_specs=[vmem, vmem],
        out_specs=(pl.BlockSpec(memory_space=pl.ANY), pl.BlockSpec(memory_space=pl.ANY)),
        scratch_shapes=[dma((9,))],
        compiler_params=pltpu.CompilerParams(vmem_limit_bytes=1 * 2**20),
        name="write_out",
    )(acc, ig)
    return wg, igo.reshape(t_loc, d_loc)


def solution(mesh):
    in_specs = (P("col", "row"), P("row", "col"), P("row", "col"), P("row", "col"))
    out_specs = (P("row", "col"), P("col", "row"))
    return jax.shard_map(local, mesh=mesh, in_specs=in_specs, out_specs=out_specs, check_vma=False)
```

```python
import functools

import jax
import jax.numpy as jnp
from jax import lax
from jax.experimental import pallas as pl
from jax.experimental.pallas import tpu as pltpu
from jax.sharding import PartitionSpec as P

BLK = 64
STEPS = 8
ROWS = 16
AHEAD = 2
LAG_YZ2, LAG_DX, LAG_SUM = 2, 2, 5
MESH = pl.DeviceIdType.MESH

M1, OWN, P1, Y, Z2, YP1, YZ2, YM1 = range(8)
CORE_GROUPS = ((0, 4), (4, 2), (6, 2))
S_ZP, S_ZM, S_Y, S_FWD, S_YZP, S_YZM, S_Y2 = range(7)


def slot_of(dz, dh):
    return ((OWN, P1, Z2, M1), (Y, YP1, YZ2, YM1))[dh][dz]


def comm_kernel(
    x_ref, dy_ref, w_ref, mask_hbm,
    acc_ref, ig_ref,
    mask_ref, dyf, xp, xt, wv, wmt, mcols, dxb, rsb, ysend, yland,
    s_piece, r_piece, s_core, r_core, s_x, r_x, s_rs, r_rs, s_half, r_half, s_y, r_y, loc,
):
    row, col = lax.axis_index("row"), lax.axis_index("col")
    core = lax.rem(row, 2)
    h = lax.rem(lax.div(row, 2), 2)
    z = lax.div(row, 4)
    x = lax.rem(col, 4)
    yl = lax.div(col, 4)

    def row_id(z_, h_, c_):
        return (z_ * 2 + h_) * 2 + c_

    zp = (row_id(lax.rem(z + 1, 4), h, core), col)
    zm = (row_id(lax.rem(z + 3, 4), h, core), col)
    yp = (row_id(z, 1 - h, core), col)
    other_core = (row_id(z, h, 1 - core), col)
    yn = (row, (1 - yl) * 4 + x)

    def xpeer(o):
        return (row, yl * 4 + lax.rem(x + o, 4))

    barrier = pltpu.get_barrier_semaphore()
    partners = [zp, zm, yp, other_core, yn, xpeer(1), xpeer(2), xpeer(3)]
    for dev in partners:
        pl.semaphore_signal(barrier, inc=1, device_id=dev, device_id_type=MESH)

    own_dy = pltpu.make_async_copy(dy_ref, dyf.at[:, core, OWN], loc.at[0])
    own_dy.start()
    w_copy = pltpu.make_async_copy(w_ref, wv, loc.at[1])
    w_copy.start()
    mask_copy = pltpu.make_async_copy(mask_hbm, mask_ref, loc.at[4])
    mask_copy.start()

    def x_slot(yl_):
        j = yl_ * 4 + x
        dz = lax.rem(lax.div(j, 2) + 4 - z, 4)
        dh = lax.rem(lax.rem(j, 2) + 2 - h, 2)
        near = lax.rem(dz + 1, 4) + lax.div(dz * (dz - 1) * (3 - dz), 2)
        far = 3 + dz + lax.div(dz + 2, 3)
        return near + dh * (far - near)

    own_x = [pltpu.make_async_copy(x_ref.at[c], xp.at[:, c, x_slot(yl)], loc.at[2 + c]) for c in range(2)]
    for cp in own_x:
        cp.start()

    pl.semaphore_wait(barrier, len(partners))

    def remote(src, dst, ss, rs, dev):
        return pltpu.make_async_remote_copy(
            src_ref=src, dst_ref=dst, send_sem=ss, recv_sem=rs, device_id=dev, device_id_type=MESH
        )

    def piece(kind, p):
        src_slot, dst_slot, dev = {
            S_ZP: (None, M1, zp),
            S_ZM: (None, P1, zm),
            S_Y: (None, Y, yp),
            S_YZP: (Y, YM1, zp),
            S_YZM: (Y, YP1, zm),
            S_Y2: (Z2, YZ2, yp),
        }[kind]
        src = dy_ref.at[p] if src_slot is None else dyf.at[p, core, src_slot]
        return remote(src, dyf.at[p, core, dst_slot], s_piece.at[kind, p], r_piece.at[dst_slot, p], dev)

    def fwd(p, up):
        src = dyf.at[p, core, M1 if up else P1]
        return remote(src, dyf.at[p, core, Z2], s_piece.at[S_FWD, p], r_piece.at[Z2, p], zp if up else zm)

    def to_core(g, p):
        lo, n = CORE_GROUPS[g]
        there = dyf.at[p, core, pl.ds(lo, n)]
        return remote(there, there, s_core.at[g, p], r_core.at[g, p], other_core)

    def from_core(g, p):
        lo, n = CORE_GROUPS[g]
        here = dyf.at[p, 1 - core, pl.ds(lo, n)]
        return remote(here, here, s_core.at[g, p], r_core.at[g, p], other_core)

    def own_sends(p):
        for kind in (S_ZP, S_ZM, S_Y):
            piece(kind, p).start()

    def x_send(o, c):
        there = xp.at[:, c, x_slot(yl)]
        return remote(x_ref.at[c], there, s_x.at[0, o, c], r_x.at[0, o, c], xpeer(o) if o else yn)

    def x_hand(o, c):
        there = xp.at[:, c, x_slot(1 - yl)]
        return remote(there, there, s_x.at[1, o, c], r_x.at[1, o, c], xpeer(o))

    dzp_own = lax.rem(lax.div(x, 2) + 4 - z, 2)
    dh_own = lax.rem(lax.rem(x, 2) + 2 - h, 2)
    cls_own = dh_own * 2 + dzp_own
    keep = lax.rem(yl + lax.div(lax.rem(z + dzp_own, 4), 2), 2)

    def cls_dest(cls):
        dh, dzp = cls // 2, cls % 2
        return 2 * lax.rem(z + dzp, 2) + lax.rem(h + dh, 2)

    def rs_send(cls, p):
        xs = cls_dest(cls)
        o = lax.rem(x + 4 - xs + 3, 4)
        return remote(dxb.at[p, cls], rsb.at[o, p], s_rs.at[cls, p], r_rs.at[o, p], (row, yl * 4 + xs))

    def rs_recv(o, p):
        return remote(rsb.at[o, p], rsb.at[o, p], s_rs.at[0, p], r_rs.at[o, p], xpeer(1))

    def rs_send_half(cls, m, p):
        xs = cls_dest(cls)
        o = lax.rem(x + 4 - xs + 3, 4)
        return remote(
            dxb.at[p, cls, m], rsb.at[o, p, m], s_half.at[cls, m], r_half.at[o, m], (row, yl * 4 + xs)
        )

    def rs_recv_half(o, m, p):
        return remote(rsb.at[o, p, m], rsb.at[o, p, m], s_half.at[0, 0], r_half.at[o, m], xpeer(1))

    def y_send(p):
        return remote(ysend.at[p], yland.at[p], s_y.at[p], r_y.at[p], yn)

    for p in range(AHEAD):
        own_sends(p)
    for c in range(2):
        for o in range(4):
            x_send(o, c).start()

    d_loc, f_loc = wv.shape
    nbr, nbc = mask_ref.shape
    tile = 512
    n_tiles = f_loc // tile
    mask_copy.wait()
    mask_bf = mask_ref[...].astype(jnp.bfloat16)

    def spread(i, _):
        cols = pl.ds(pl.multiple_of(i * tile, tile), tile)
        block = lax.broadcasted_iota(jnp.int32, (nbc, tile), 0)
        first = block * BLK - i * tile
        lane = lax.broadcasted_iota(jnp.int32, (nbc, tile), 1)
        hit = jnp.logical_and(lane >= first, lane < first + BLK)
        pick = jnp.where(hit, 1.0, 0.0).astype(jnp.bfloat16)
        mcols[:, cols] = jnp.dot(mask_bf, pick, preferred_element_type=jnp.float32)
        return 0

    lax.fori_loop(0, n_tiles, spread, 0)
    w_copy.wait()

    def mask_w(i, _):
        cols = pl.ds(pl.multiple_of(i * tile, tile), tile)
        upper = lax.broadcasted_iota(jnp.int32, (2 * BLK, tile), 0) < BLK
        for b in range(d_loc // (2 * BLK)):
            m = jnp.where(upper, mcols[2 * b : 2 * b + 1, cols], mcols[2 * b + 1 : 2 * b + 2, cols])
            wm = wv[b * 2 * BLK : (b + 1) * 2 * BLK, cols] * m.astype(jnp.bfloat16)
            wmt[cols, b * 2 * BLK : (b + 1) * 2 * BLK] = wm.T
        return 0

    lax.fori_loop(0, n_tiles, mask_w, 0)
    own_dy.wait()

    def wgrad(b, first, last, lo=0, hi=2):
        wide = f_loc // 2
        span = xt.shape[1]
        if lo == 0:
            xt[...] = xp[pl.ds(2 * b, 2)].reshape(span, d_loc).T

        def one(i, _):
            cols = pl.ds(pl.multiple_of(i * wide, wide), wide)
            dy2 = dyf[pl.ds(2 * b, 2), :, :, :, cols].reshape(span, wide)
            part = jnp.dot(xt[...], dy2, preferred_element_type=jnp.float32)
            if not first:
                part = part + acc_ref[:, cols]
            if last:
                for i_b in range(nbr):
                    rows = slice(i_b * BLK, (i_b + 1) * BLK)
                    acc_ref[rows, cols] = part[rows] * mcols[i_b : i_b + 1, cols]
            else:
                acc_ref[:, cols] = part
            return 0

        lax.fori_loop(lo, hi, one, 0)

    def dx_rows(q, lo, n):
        part = jnp.dot(
            dyf[q, :, lo : lo + n].reshape(2 * n * ROWS, f_loc), wmt[...], preferred_element_type=jnp.float32
        ).astype(jnp.bfloat16)
        for cls in range(4):
            dh, dzp = cls // 2, cls % 2
            for m in range(2):
                slot = slot_of(dzp + 2 * m, dh)
                if not lo <= slot < lo + n:
                    continue
                for c in range(2):
                    at = (c * n + slot - lo) * ROWS
                    dxb[q, cls, m, c] = part[at : at + ROWS]
                if n < 8:

                    @pl.when(cls_dest(cls) != x)
                    def _():
                        rs_send_half(cls, m, q).start()

    def dx_step(q):
        for g in range(3):
            from_core(g, q).wait_recv()
        dx_rows(q, 0, 8)
        for cls in range(4):

            @pl.when(cls_dest(cls) != x)
            def _():
                rs_send(cls, q).start()

    def rs_total(q, m):
        t = dxb[q, cls_own, m].astype(jnp.float32)
        for o in range(3):
            t = t + rsb[o, q, m].astype(jnp.float32)
        return t

    def rs_wait(q, m):
        for o in range(3):
            if isinstance(q, int) and q == STEPS - 1:
                rs_recv_half(o, m, q).wait_recv()
            else:
                rs_recv(o, q).wait_recv()

    def rs_along_y(q):
        rs_wait(q, 1 - keep)
        ysend[q] = rs_total(q, 1 - keep).astype(jnp.bfloat16)
        y_send(q).start()

    def rs_finish(q):
        if isinstance(q, int) and q == STEPS - 1:
            rs_wait(q, keep)
        t = rs_total(q, keep)
        y_send(q).wait_recv()
        t = (t + yland[q].astype(jnp.float32)).astype(jnp.bfloat16)
        for c in range(2):
            ig_ref[c, q] = t[c]

    def neighbours(p, more):
        piece(S_ZP, p).wait_recv()
        piece(S_ZM, p).wait_recv()

        @pl.when(lax.rem(p, 2) == 0)
        def _():
            fwd(p, True).start()

        @pl.when(lax.rem(p, 2) == 1)
        def _():
            fwd(p, False).start()

        piece(S_Y, p).wait_recv()
        piece(S_YZP, p).start()
        piece(S_YZM, p).start()
        to_core(0, p).start()

        @pl.when(more)
        def _():
            own_sends(p + AHEAD)

    def second(p):
        fwd(p, True).wait_recv()
        piece(S_Y2, p).start()

    def second_core(p):
        piece(S_YZM, p).wait_recv()
        to_core(1, p).start()

    def third(p):
        piece(S_YZP, p).wait_recv()
        piece(S_Y2, p).wait_recv()
        to_core(2, p).start()

    def step(s, _):
        neighbours(s, s < STEPS - AHEAD)

        @pl.when(s == 0)
        def _():
            for c in range(2):
                x_send(0, c).wait_recv()
                for o in range(1, 4):
                    x_hand(o, c).start()

        @pl.when(s >= LAG_YZ2)
        def _():
            third(s - LAG_YZ2)

        @pl.when(s >= 1)
        def _():
            second(s - 1)
            second_core(s - 1)

        @pl.when(s >= LAG_DX)
        def _():
            q = s - LAG_DX
            dx_step(q)

            @pl.when(q == 2)
            def _():
                for c in range(2):
                    own_x[c].wait()
                    for o in range(1, 4):
                        x_send(o, c).wait_recv()
                        x_hand(o, c).wait_recv()
                wgrad(0, True, False)

            @pl.when(q == 3)
            def _():
                wgrad(1, False, False, 0, 1)

            @pl.when(q == 4)
            def _():
                wgrad(1, False, False, 1, 2)

        @pl.when(s >= LAG_SUM)
        def _():
            rs_along_y(s - LAG_SUM)

        return 0

    lax.fori_loop(0, STEPS, step, 0)
    last = STEPS - 1
    wgrad(2, False, False)
    third(last - 1)
    second(last)
    second_core(last)
    dx_step(last - 1)
    from_core(0, last).wait_recv()
    dx_rows(last, 0, 4)
    third(last)
    for q in range(STEPS - LAG_SUM, last - 1):
        rs_along_y(q)
    for q in range(STEPS - LAG_SUM):
        rs_finish(q)
    from_core(1, last).wait_recv()
    from_core(2, last).wait_recv()
    dx_rows(last, 4, 4)
    rs_along_y(last - 1)
    for q in range(STEPS - LAG_SUM, last - 1):
        rs_finish(q)
    wgrad(3, False, True, 0, 1)
    rs_along_y(last)
    rs_finish(last - 1)
    wgrad(3, False, True, 1, 2)
    rs_finish(last)

    def drain(p, _):
        for kind in (S_ZP, S_ZM, S_Y, S_YZP, S_YZM, S_Y2):
            piece(kind, p).wait_send()
        fwd(p, True).wait_send()
        for g in range(3):
            to_core(g, p).wait_send()
        y_send(p).wait_send()
        return 0

    def drain_rs(p, _):
        for cls in range(4):

            @pl.when(cls_dest(cls) != x)
            def _():
                rs_send(cls, p).wait_send()

        return 0

    lax.fori_loop(0, STEPS, drain, 0)
    lax.fori_loop(0, STEPS - 1, drain_rs, 0)
    for cls in range(4):

        @pl.when(cls_dest(cls) != x)
        def _():
            for m in range(2):
                rs_send_half(cls, m, STEPS - 1).wait_send()

    for c in range(2):
        for o in range(4):
            x_send(o, c).wait_send()
            if o:
                x_hand(o, c).wait_send()


def write_kernel(acc_ref, ig_ref, wg_ref, ig_out, sems):
    parts = 8
    rows = acc_ref.shape[0] // parts
    copies = [pltpu.make_async_copy(ig_ref, ig_out, sems.at[parts])]
    for i in range(parts):
        part = pl.ds(i * rows, rows)
        copies.append(pltpu.make_async_copy(acc_ref.at[part], wg_ref.at[part], sems.at[i]))
    for cp in copies:
        cp.start()
    for cp in copies:
        cp.wait()


def local(activations, out_grad, weight, block_mask):
    t_loc, d_loc = activations.shape
    s_loc, f_loc = out_grad.shape
    bf, f32 = jnp.bfloat16, jnp.float32
    dma = pltpu.SemaphoreType.DMA
    hbm = pl.BlockSpec(memory_space=pltpu.HBM)
    vmem = pl.BlockSpec(memory_space=pltpu.VMEM)
    acc, ig = pl.pallas_call(
        comm_kernel,
        out_shape=(
            pltpu.VMEM((d_loc, f_loc), f32),
            pltpu.VMEM((2, STEPS, ROWS, d_loc), bf),
        ),
        in_specs=[hbm] * 4,
        out_specs=(vmem, vmem),
        scratch_shapes=[
            pltpu.VMEM(block_mask.shape, jnp.int32),
            pltpu.VMEM((STEPS, 2, 8, ROWS, f_loc), bf),
            pltpu.VMEM((STEPS, 2, 8, ROWS, d_loc), bf),
            pltpu.VMEM((d_loc, 32 * ROWS), bf),
            pltpu.VMEM((d_loc, f_loc), bf),
            pltpu.VMEM((f_loc, d_loc), bf),
            pltpu.VMEM((block_mask.shape[0], f_loc), f32),
            pltpu.VMEM((STEPS, 4, 2, 2, ROWS, d_loc), bf),
            pltpu.VMEM((3, STEPS, 2, 2, ROWS, d_loc), bf),
            pltpu.VMEM((STEPS, 2, ROWS, d_loc), bf),
            pltpu.VMEM((STEPS, 2, ROWS, d_loc), bf),
            dma((7, STEPS)),
            dma((8, STEPS)),
            dma((3, STEPS)),
            dma((3, STEPS)),
            dma((2, 4, 2)),
            dma((2, 4, 2)),
            dma((4, STEPS)),
            dma((3, STEPS)),
            dma((4, 2)),
            dma((3, 2)),
            dma((STEPS,)),
            dma((STEPS,)),
            dma((5,)),
        ],
        compiler_params=pltpu.CompilerParams(
            collective_id=0, has_side_effects=True, vmem_limit_bytes=46 * 2**20
        ),
        name="gather_multiply_reduce",
    )(
        *(
            pltpu.with_memory_space_constraint(a, pltpu.HBM)
            for a in (
                activations.reshape(2, STEPS, ROWS, d_loc),
                out_grad.reshape(STEPS, ROWS, f_loc),
                weight,
                block_mask,
            )
        )
    )
    wg, igo = pl.pallas_call(
        write_kernel,
        out_shape=(
            jax.ShapeDtypeStruct((d_loc, f_loc), f32),
            jax.ShapeDtypeStruct((2, STEPS, ROWS, d_loc), bf),
        ),
        in_specs=[vmem, vmem],
        out_specs=(pl.BlockSpec(memory_space=pl.ANY), pl.BlockSpec(memory_space=pl.ANY)),
        scratch_shapes=[dma((9,))],
        compiler_params=pltpu.CompilerParams(vmem_limit_bytes=1 * 2**20),
        name="write_out",
    )(acc, ig)
    return wg, igo.reshape(t_loc, d_loc)


def solution(mesh):
    in_specs = (P("col", "row"), P("row", "col"), P("row", "col"), P("row", "col"))
    out_specs = (P("row", "col"), P("col", "row"))
    return jax.shard_map(local, mesh=mesh, in_specs=in_specs, out_specs=out_specs, check_vma=False)
```

```python
import functools

import jax
import jax.numpy as jnp
from jax import lax
from jax.experimental import pallas as pl
from jax.experimental.pallas import tpu as pltpu
from jax.sharding import PartitionSpec as P

BLK = 64
STEPS = 8
ROWS = 16
AHEAD = 2
LAG_YZ2, LAG_DX, LAG_SUM = 2, 2, 5
MESH = pl.DeviceIdType.MESH

M1, OWN, P1, Y, Z2, YP1, YZ2, YM1 = range(8)
CORE_GROUPS = ((0, 4), (4, 2), (6, 2))
S_ZP, S_ZM, S_Y, S_FWD, S_YZP, S_YZM, S_Y2 = range(7)


def slot_of(dz, dh):
    return ((OWN, P1, Z2, M1), (Y, YP1, YZ2, YM1))[dh][dz]


def comm_kernel(
    x_ref, dy_ref, w_ref, mask_hbm,
    acc_ref, ig_ref,
    mask_ref, dyf, xp, xt, wv, wmt, mcols, dxb, rsb, ysend, yland,
    s_piece, r_piece, s_core, r_core, s_x, r_x, s_rs, r_rs, s_half, r_half, s_y, r_y, loc,
):
    row, col = lax.axis_index("row"), lax.axis_index("col")
    core = lax.rem(row, 2)
    h = lax.rem(lax.div(row, 2), 2)
    z = lax.div(row, 4)
    x = lax.rem(col, 4)
    yl = lax.div(col, 4)

    def row_id(z_, h_, c_):
        return (z_ * 2 + h_) * 2 + c_

    zp = (row_id(lax.rem(z + 1, 4), h, core), col)
    zm = (row_id(lax.rem(z + 3, 4), h, core), col)
    yp = (row_id(z, 1 - h, core), col)
    other_core = (row_id(z, h, 1 - core), col)
    yn = (row, (1 - yl) * 4 + x)

    def xpeer(o):
        return (row, yl * 4 + lax.rem(x + o, 4))

    barrier = pltpu.get_barrier_semaphore()
    partners = [zp, zm, yp, other_core, yn, xpeer(1), xpeer(2), xpeer(3)]
    for dev in partners:
        pl.semaphore_signal(barrier, inc=1, device_id=dev, device_id_type=MESH)

    own_dy = pltpu.make_async_copy(dy_ref, dyf.at[:, core, OWN], loc.at[0])
    own_dy.start()
    w_copy = pltpu.make_async_copy(w_ref, wv, loc.at[1])
    w_copy.start()
    mask_copy = pltpu.make_async_copy(mask_hbm, mask_ref, loc.at[4])
    mask_copy.start()

    def x_slot(yl_):
        j = yl_ * 4 + x
        dz = lax.rem(lax.div(j, 2) + 4 - z, 4)
        dh = lax.rem(lax.rem(j, 2) + 2 - h, 2)
        near = lax.rem(dz + 1, 4) + lax.div(dz * (dz - 1) * (3 - dz), 2)
        far = 3 + dz + lax.div(dz + 2, 3)
        return near + dh * (far - near)

    own_x = [pltpu.make_async_copy(x_ref.at[c], xp.at[:, c, x_slot(yl)], loc.at[2 + c]) for c in range(2)]
    for cp in own_x:
        cp.start()

    pl.semaphore_wait(barrier, len(partners))

    def remote(src, dst, ss, rs, dev):
        return pltpu.make_async_remote_copy(
            src_ref=src, dst_ref=dst, send_sem=ss, recv_sem=rs, device_id=dev, device_id_type=MESH
        )

    def piece(kind, p):
        src_slot, dst_slot, dev = {
            S_ZP: (None, M1, zp),
            S_ZM: (None, P1, zm),
            S_Y: (None, Y, yp),
            S_YZP: (Y, YM1, zp),
            S_YZM: (Y, YP1, zm),
            S_Y2: (Z2, YZ2, yp),
        }[kind]
        src = dy_ref.at[p] if src_slot is None else dyf.at[p, core, src_slot]
        return remote(src, dyf.at[p, core, dst_slot], s_piece.at[kind, p], r_piece.at[dst_slot, p], dev)

    def fwd(p, up):
        src = dyf.at[p, core, M1 if up else P1]
        return remote(src, dyf.at[p, core, Z2], s_piece.at[S_FWD, p], r_piece.at[Z2, p], zp if up else zm)

    def to_core(g, p):
        lo, n = CORE_GROUPS[g]
        there = dyf.at[p, core, pl.ds(lo, n)]
        return remote(there, there, s_core.at[g, p], r_core.at[g, p], other_core)

    def from_core(g, p):
        lo, n = CORE_GROUPS[g]
        here = dyf.at[p, 1 - core, pl.ds(lo, n)]
        return remote(here, here, s_core.at[g, p], r_core.at[g, p], other_core)

    def own_sends(p):
        for kind in (S_ZP, S_ZM, S_Y):
            piece(kind, p).start()

    def x_send(o, c):
        there = xp.at[:, c, x_slot(yl)]
        return remote(x_ref.at[c], there, s_x.at[0, o, c], r_x.at[0, o, c], xpeer(o) if o else yn)

    def x_hand(o, c):
        there = xp.at[:, c, x_slot(1 - yl)]
        return remote(there, there, s_x.at[1, o, c], r_x.at[1, o, c], xpeer(o))

    dzp_own = lax.rem(lax.div(x, 2) + 4 - z, 2)
    dh_own = lax.rem(lax.rem(x, 2) + 2 - h, 2)
    cls_own = dh_own * 2 + dzp_own
    keep = lax.rem(yl + lax.div(lax.rem(z + dzp_own, 4), 2), 2)

    def cls_dest(cls):
        dh, dzp = cls // 2, cls % 2
        return 2 * lax.rem(z + dzp, 2) + lax.rem(h + dh, 2)

    def rs_send(cls, p):
        xs = cls_dest(cls)
        o = lax.rem(x + 4 - xs + 3, 4)
        return remote(dxb.at[p, cls], rsb.at[o, p], s_rs.at[cls, p], r_rs.at[o, p], (row, yl * 4 + xs))

    def rs_recv(o, p):
        return remote(rsb.at[o, p], rsb.at[o, p], s_rs.at[0, p], r_rs.at[o, p], xpeer(1))

    def rs_send_half(cls, m, p):
        xs = cls_dest(cls)
        o = lax.rem(x + 4 - xs + 3, 4)
        return remote(
            dxb.at[p, cls, m], rsb.at[o, p, m], s_half.at[cls, m], r_half.at[o, m], (row, yl * 4 + xs)
        )

    def rs_recv_half(o, m, p):
        return remote(rsb.at[o, p, m], rsb.at[o, p, m], s_half.at[0, 0], r_half.at[o, m], xpeer(1))

    def y_send(p):
        return remote(ysend.at[p], yland.at[p], s_y.at[p], r_y.at[p], yn)

    for p in range(AHEAD):
        own_sends(p)
    for c in range(2):
        for o in range(4):
            x_send(o, c).start()

    d_loc, f_loc = wv.shape
    nbr, nbc = mask_ref.shape
    tile = 512
    n_tiles = f_loc // tile
    mask_copy.wait()
    mask_bf = mask_ref[...].astype(jnp.bfloat16)

    def spread(i, _):
        cols = pl.ds(pl.multiple_of(i * tile, tile), tile)
        block = lax.broadcasted_iota(jnp.int32, (nbc, tile), 0)
        first = block * BLK - i * tile
        lane = lax.broadcasted_iota(jnp.int32, (nbc, tile), 1)
        hit = jnp.logical_and(lane >= first, lane < first + BLK)
        pick = jnp.where(hit, 1.0, 0.0).astype(jnp.bfloat16)
        mcols[:, cols] = jnp.dot(mask_bf, pick, preferred_element_type=jnp.float32)
        return 0

    lax.fori_loop(0, n_tiles, spread, 0)
    w_copy.wait()

    def mask_w(i, _):
        cols = pl.ds(pl.multiple_of(i * tile, tile), tile)
        upper = lax.broadcasted_iota(jnp.int32, (2 * BLK, tile), 0) < BLK
        for b in range(d_loc // (2 * BLK)):
            m = jnp.where(upper, mcols[2 * b : 2 * b + 1, cols], mcols[2 * b + 1 : 2 * b + 2, cols])
            wm = wv[b * 2 * BLK : (b + 1) * 2 * BLK, cols] * m.astype(jnp.bfloat16)
            wmt[cols, b * 2 * BLK : (b + 1) * 2 * BLK] = wm.T
        return 0

    lax.fori_loop(0, n_tiles, mask_w, 0)
    own_dy.wait()

    def wgrad(b, first, last, lo=0, hi=2):
        wide = f_loc // 2
        span = xt.shape[1]
        if lo == 0:
            xt[...] = xp[pl.ds(2 * b, 2)].reshape(span, d_loc).T

        def one(i, _):
            cols = pl.ds(pl.multiple_of(i * wide, wide), wide)
            dy2 = dyf[pl.ds(2 * b, 2), :, :, :, cols].reshape(span, wide)
            part = jnp.dot(xt[...], dy2, preferred_element_type=jnp.float32)
            if not first:
                part = part + acc_ref[:, cols]
            if last:
                for i_b in range(nbr):
                    rows = slice(i_b * BLK, (i_b + 1) * BLK)
                    acc_ref[rows, cols] = part[rows] * mcols[i_b : i_b + 1, cols]
            else:
                acc_ref[:, cols] = part
            return 0

        lax.fori_loop(lo, hi, one, 0)

    def dx_rows(q, lo, n):
        part = jnp.dot(
            dyf[q, :, lo : lo + n].reshape(2 * n * ROWS, f_loc), wmt[...], preferred_element_type=jnp.float32
        ).astype(jnp.bfloat16)
        for cls in range(4):
            dh, dzp = cls // 2, cls % 2
            for m in range(2):
                slot = slot_of(dzp + 2 * m, dh)
                if not lo <= slot < lo + n:
                    continue
                for c in range(2):
                    at = (c * n + slot - lo) * ROWS
                    dxb[q, cls, m, c] = part[at : at + ROWS]
                if n < 8:

                    @pl.when(cls_dest(cls) != x)
                    def _():
                        rs_send_half(cls, m, q).start()

    def dx_step(q):
        for g in range(3):
            from_core(g, q).wait_recv()
        dx_rows(q, 0, 8)
        for cls in range(4):

            @pl.when(cls_dest(cls) != x)
            def _():
                rs_send(cls, q).start()

    def rs_total(q, m):
        t = dxb[q, cls_own, m].astype(jnp.float32)
        for o in range(3):
            t = t + rsb[o, q, m].astype(jnp.float32)
        return t

    def rs_wait(q, m):
        for o in range(3):
            if isinstance(q, int) and q == STEPS - 1:
                rs_recv_half(o, m, q).wait_recv()
            else:
                rs_recv(o, q).wait_recv()

    def rs_along_y(q):
        rs_wait(q, 1 - keep)
        ysend[q] = rs_total(q, 1 - keep).astype(jnp.bfloat16)
        y_send(q).start()

    def rs_finish(q):
        if isinstance(q, int) and q == STEPS - 1:
            rs_wait(q, keep)
        t = rs_total(q, keep)
        y_send(q).wait_recv()
        t = (t + yland[q].astype(jnp.float32)).astype(jnp.bfloat16)
        for c in range(2):
            ig_ref[c, q] = t[c]

    def neighbours(p, more):
        piece(S_ZP, p).wait_recv()
        piece(S_ZM, p).wait_recv()

        @pl.when(lax.rem(p, 2) == 0)
        def _():
            fwd(p, True).start()

        @pl.when(lax.rem(p, 2) == 1)
        def _():
            fwd(p, False).start()

        piece(S_Y, p).wait_recv()
        piece(S_YZP, p).start()
        piece(S_YZM, p).start()
        to_core(0, p).start()

        @pl.when(more)
        def _():
            own_sends(p + AHEAD)

    def second(p):
        fwd(p, True).wait_recv()
        piece(S_Y2, p).start()

    def second_core(p):
        piece(S_YZM, p).wait_recv()
        to_core(1, p).start()

    def third(p):
        piece(S_YZP, p).wait_recv()
        piece(S_Y2, p).wait_recv()
        to_core(2, p).start()

    def step(s, _):
        neighbours(s, s < STEPS - AHEAD)

        @pl.when(s >= LAG_YZ2)
        def _():
            third(s - LAG_YZ2)

        @pl.when(s >= 1)
        def _():
            second(s - 1)
            second_core(s - 1)

        @pl.when(s == 1)
        def _():
            for c in range(2):
                x_send(0, c).wait_recv()
                for o in range(1, 4):
                    x_hand(o, c).start()

        @pl.when(s >= LAG_DX)
        def _():
            q = s - LAG_DX
            dx_step(q)

            @pl.when(q == 2)
            def _():
                for c in range(2):
                    own_x[c].wait()
                    for o in range(1, 4):
                        x_send(o, c).wait_recv()
                        x_hand(o, c).wait_recv()
                wgrad(0, True, False)

            @pl.when(q == 3)
            def _():
                wgrad(1, False, False, 0, 1)

            @pl.when(q == 4)
            def _():
                wgrad(1, False, False, 1, 2)

        @pl.when(s >= LAG_SUM)
        def _():
            rs_along_y(s - LAG_SUM)

        return 0

    lax.fori_loop(0, STEPS, step, 0)
    last = STEPS - 1
    wgrad(2, False, False)
    third(last - 1)
    second(last)
    second_core(last)
    dx_step(last - 1)
    from_core(0, last).wait_recv()
    dx_rows(last, 0, 4)
    third(last)
    for q in range(STEPS - LAG_SUM, last - 1):
        rs_along_y(q)
    for q in range(STEPS - LAG_SUM):
        rs_finish(q)
    from_core(1, last).wait_recv()
    from_core(2, last).wait_recv()
    dx_rows(last, 4, 4)
    rs_along_y(last - 1)
    for q in range(STEPS - LAG_SUM, last - 1):
        rs_finish(q)
    wgrad(3, False, True, 0, 1)
    rs_along_y(last)
    rs_finish(last - 1)
    wgrad(3, False, True, 1, 2)
    rs_finish(last)

    def drain(p, _):
        for kind in (S_ZP, S_ZM, S_Y, S_YZP, S_YZM, S_Y2):
            piece(kind, p).wait_send()
        fwd(p, True).wait_send()
        for g in range(3):
            to_core(g, p).wait_send()
        y_send(p).wait_send()
        return 0

    def drain_rs(p, _):
        for cls in range(4):

            @pl.when(cls_dest(cls) != x)
            def _():
                rs_send(cls, p).wait_send()

        return 0

    lax.fori_loop(0, STEPS, drain, 0)
    lax.fori_loop(0, STEPS - 1, drain_rs, 0)
    for cls in range(4):

        @pl.when(cls_dest(cls) != x)
        def _():
            for m in range(2):
                rs_send_half(cls, m, STEPS - 1).wait_send()

    for c in range(2):
        for o in range(4):
            x_send(o, c).wait_send()
            if o:
                x_hand(o, c).wait_send()


def write_kernel(acc_ref, ig_ref, wg_ref, ig_out, sems):
    parts = 8
    rows = acc_ref.shape[0] // parts
    copies = [pltpu.make_async_copy(ig_ref, ig_out, sems.at[parts])]
    for i in range(parts):
        part = pl.ds(i * rows, rows)
        copies.append(pltpu.make_async_copy(acc_ref.at[part], wg_ref.at[part], sems.at[i]))
    for cp in copies:
        cp.start()
    for cp in copies:
        cp.wait()


def local(activations, out_grad, weight, block_mask):
    t_loc, d_loc = activations.shape
    s_loc, f_loc = out_grad.shape
    bf, f32 = jnp.bfloat16, jnp.float32
    dma = pltpu.SemaphoreType.DMA
    hbm = pl.BlockSpec(memory_space=pltpu.HBM)
    vmem = pl.BlockSpec(memory_space=pltpu.VMEM)
    acc, ig = pl.pallas_call(
        comm_kernel,
        out_shape=(
            pltpu.VMEM((d_loc, f_loc), f32),
            pltpu.VMEM((2, STEPS, ROWS, d_loc), bf),
        ),
        in_specs=[hbm] * 4,
        out_specs=(vmem, vmem),
        scratch_shapes=[
            pltpu.VMEM(block_mask.shape, jnp.int32),
            pltpu.VMEM((STEPS, 2, 8, ROWS, f_loc), bf),
            pltpu.VMEM((STEPS, 2, 8, ROWS, d_loc), bf),
            pltpu.VMEM((d_loc, 32 * ROWS), bf),
            pltpu.VMEM((d_loc, f_loc), bf),
            pltpu.VMEM((f_loc, d_loc), bf),
            pltpu.VMEM((block_mask.shape[0], f_loc), f32),
            pltpu.VMEM((STEPS, 4, 2, 2, ROWS, d_loc), bf),
            pltpu.VMEM((3, STEPS, 2, 2, ROWS, d_loc), bf),
            pltpu.VMEM((STEPS, 2, ROWS, d_loc), bf),
            pltpu.VMEM((STEPS, 2, ROWS, d_loc), bf),
            dma((7, STEPS)),
            dma((8, STEPS)),
            dma((3, STEPS)),
            dma((3, STEPS)),
            dma((2, 4, 2)),
            dma((2, 4, 2)),
            dma((4, STEPS)),
            dma((3, STEPS)),
            dma((4, 2)),
            dma((3, 2)),
            dma((STEPS,)),
            dma((STEPS,)),
            dma((5,)),
        ],
        compiler_params=pltpu.CompilerParams(
            collective_id=0, has_side_effects=True, vmem_limit_bytes=46 * 2**20
        ),
        name="gather_multiply_reduce",
    )(
        *(
            pltpu.with_memory_space_constraint(a, pltpu.HBM)
            for a in (
                activations.reshape(2, STEPS, ROWS, d_loc),
                out_grad.reshape(STEPS, ROWS, f_loc),
                weight,
                block_mask,
            )
        )
    )
    wg, igo = pl.pallas_call(
        write_kernel,
        out_shape=(
            jax.ShapeDtypeStruct((d_loc, f_loc), f32),
            jax.ShapeDtypeStruct((2, STEPS, ROWS, d_loc), bf),
        ),
        in_specs=[vmem, vmem],
        out_specs=(pl.BlockSpec(memory_space=pl.ANY), pl.BlockSpec(memory_space=pl.ANY)),
        scratch_shapes=[dma((9,))],
        compiler_params=pltpu.CompilerParams(vmem_limit_bytes=1 * 2**20),
        name="write_out",
    )(acc, ig)
    return wg, igo.reshape(t_loc, d_loc)


def solution(mesh):
    in_specs = (P("col", "row"), P("row", "col"), P("row", "col"), P("row", "col"))
    out_specs = (P("row", "col"), P("col", "row"))
    return jax.shard_map(local, mesh=mesh, in_specs=in_specs, out_specs=out_specs, check_vma=False)
```
